256 devices in a mesh: rows: 8 (over y, core), cols: 32 (over x, z).
Axes of the slice: x: 4, y: 4, z: 8, core: 2. Of those that a mesh axis runs over, the one named last changes fastest.
Arguments:
- out_grad: bfloat16 [2048, 8192], P('rows', 'cols'), may hold values from -6 to 6
- gate_act: bfloat16 [2048, 28672], P('cols', 'rows'), may hold values from -8 to 8
- up_act: bfloat16 [2048, 28672], P('cols', 'rows'), may hold values from -6 to 6
- down_weight: bfloat16 [28672, 8192], P('rows', 'cols'), may hold values from -0.03125 to 0.03125
Outputs:
- weight_grad: float32 [28672, 8192], P('rows', 'cols')
- gate_grad: bfloat16 [2048, 28672], P('cols', 'rows')
- up_grad: bfloat16 [2048, 28672], P('cols', 'rows')
The draws below stay inside these ranges and needn't reach their ends.
All inputs are finite; a program needn't handle non-finite values.
Results may differ from the reference program's by a relative error of at most 0.034.
Values may be sent and summed in bfloat16 or wider, within the bound.
A program may use at most 128 MiB of HBM per device.

```python
import jax
import jax.numpy as jnp
from jax import lax

D = 8192
FF = 28672
TOKENS = 2048
N_COLS = 32


def spiked(array, rng, source, target, parts, factor):
    owner, partner = [(jnp.arange(array.shape[position]) // (array.shape[position] // parts)).reshape([-1 if axis == position else 1 for axis in range(array.ndim)]) for position in (source, target)]
    chosen = jax.random.permutation(rng, parts)[partner]
    strong = (owner == chosen) | (owner == (partner + parts // 2) % parts)
    return jnp.where(strong, factor * array, array)


def block_scale(stream_key, extent, cuts, smallest, largest):
    def one(dim, parts):
        draws = jax.random.uniform(jax.random.fold_in(jax.random.fold_in(stream_key, 6), dim), (parts,), jnp.float32, smallest / len(cuts), largest / len(cuts))
        return jnp.repeat(jnp.exp(draws), extent[dim] // parts).reshape((-1,) + (1,) * (len(extent) - dim - 1))

    level = one(*cuts[0])
    for cut in cuts[1:]:
        level = level * one(*cut)
    return level


def scatter_about(stream_key, extent, deviation, reach, split=(), held_as=jnp.bfloat16):
    drawn = jax.random.normal(stream_key, extent, jnp.float32) * deviation
    if len(split) > 0:
        drawn = block_scale(stream_key, extent, split, -0.22, 0.18) * drawn
    return jnp.clip(drawn, min=-reach, max=reach).astype(held_as)


def heavy_noise(own_key, dims, width, reach, pieces, heavy, held_as=jnp.bfloat16):
    entries = width * jax.random.normal(own_key, dims, jnp.float32)
    if pieces:
        entries = entries * block_scale(own_key, dims, pieces, -0.22, 0.18)
    return jnp.clip(spiked(entries, jax.random.fold_in(own_key, 3), *heavy), -reach, reach).astype(held_as)


def setup_inputs(seed: int = 0) -> dict:
    key_of = jax.random.split(jax.random.key(seed), 5)
    return {
        "out_grad": heavy_noise(key_of[0], (TOKENS, D), 1.0, 6.0, ((0, 8), (1, 32)), (1, 0, 32, 2.75)),
        "gate_act": scatter_about(key_of[1], (TOKENS, FF), 1.5, 8.0, ((0, 32), (1, 8))),
        "up_act": scatter_about(key_of[2], (TOKENS, FF), 1.0, 6.0, ((0, 32), (1, 8))),
        "down_weight": scatter_about(key_of[3], (FF, D), FF ** -0.5, 0.03125, ((0, 8), (1, 32))),
    }


def reference(out_grad, gate_act, up_act, down_weight):
    gate_wide = gate_act.astype(jnp.float32)
    up_wide = up_act.astype(jnp.float32)
    sigmoid_gate = jax.nn.sigmoid(gate_wide)
    swish = gate_wide * sigmoid_gate
    hidden = (swish * up_wide).astype(jnp.bfloat16)
    group_width = D // N_COLS
    grad_groups = out_grad.reshape(TOKENS, N_COLS, group_width).transpose(1, 0, 2)
    weight_groups = down_weight.reshape(FF, N_COLS, group_width).transpose(1, 0, 2)

    def add_group(running, operands):
        partial_value = lax.dot_general(operands[0], operands[1], (((1,), (1,)), ((), ())),
                                  preferred_element_type=jnp.float32)
        rounded = lax.optimization_barrier(partial_value.astype(jnp.bfloat16))
        return running + rounded.astype(jnp.float32), None

    hidden_grad, _ = lax.scan(add_group, jnp.zeros((TOKENS, FF), jnp.float32),
                              (grad_groups, weight_groups))
    gate_grad = (hidden_grad * up_wide * sigmoid_gate * (1.0 + gate_wide * (1.0 - sigmoid_gate))).astype(jnp.bfloat16)
    up_grad = (hidden_grad * swish).astype(jnp.bfloat16)
    weight_grad = lax.dot_general(hidden, out_grad, (((0,), (0,)), ((), ())),
                                  preferred_element_type=jnp.float32)
    return weight_grad, gate_grad, up_grad
```

```python
import jax
import jax.numpy as jnp
from jax import lax
from jax.experimental import pallas as pl
from jax.experimental.pallas import tpu as pltpu
from jax.sharding import PartitionSpec as P

MESH = pl.DeviceIdType.MESH
NX, NY, NZ = 4, 4, 8
TOK = 64
SUB = 896
DB = 256
DG = NX * DB
BLK = NX * TOK
HALF = BLK // 2
R, L = 0, 1


def kernel(
    g, gate, up, w, hs_out, dw_out,
    gate_v, up_v, hid, hh, hht, gg, wg, part, rs_send, rs_recv, fin, acc, dws,
    lsem, hs_s, hs_r, gx_s, gx_r, gy_s, gy_r, gc_s, gc_r, w_s, w_r,
    ag_s, ag_r, rs_s, rs_r, f_s, f_r, dw_s, dw_r,
):
    r, c = lax.axis_index("rows"), lax.axis_index("cols")
    y, core, x, z = r // 2, r % 2, c // NZ, c % NZ

    def dev(dx=0, dz=0, dy=0, dc=0):
        return (
            ((y + dy) % NY) * 2 + (core + dc) % 2,
            ((x + dx) % NX) * NZ + (z + dz + NZ) % NZ,
        )

    def remote(src, dst, s, d, to):
        return pltpu.make_async_remote_copy(
            src_ref=src, dst_ref=dst, send_sem=s, recv_sem=d, device_id=to, device_id_type=MESH
        )

    def at(i, n):
        return pl.ds(pl.multiple_of(i * n, n), n)

    peers = [dev(dx=1), dev(dx=2), dev(dx=3), dev(dy=1), dev(dy=2), dev(dy=3), dev(dc=1), dev(dz=1), dev(dz=-1)]
    barrier = pltpu.get_barrier_semaphore()
    for peer in peers:
        pl.semaphore_signal(barrier, inc=1, device_id=peer, device_id_type=MESH)

    load_gate = pltpu.make_async_copy(gate, gate_v, lsem.at[0])
    load_up = pltpu.make_async_copy(up, up_v, lsem.at[1])
    load_g = pltpu.make_async_copy(g, gg.at[at(core, 4), at(y, TOK), at(x, DB)], lsem.at[2])
    load_w = pltpu.make_async_copy(w.at[at(x, SUB)], wg.at[:, at(x, DB)], lsem.at[3])
    load_gate.start()
    load_up.start()
    load_g.start()
    load_w.start()
    load_gate.wait()
    load_up.wait()
    for q in range(NX):
        cols = slice(q * SUB, (q + 1) * SUB)
        wide = gate_v[:, cols].astype(jnp.float32)
        swish = wide * jax.nn.sigmoid(wide)
        hid[q] = (swish * up_v[:, cols].astype(jnp.float32)).astype(jnp.bfloat16)
    pl.semaphore_wait(barrier, len(peers))

    sent = []

    def go(copy):
        copy.start()
        sent.append(copy)
        return copy

    hid_copies = []
    for d in (2, 1, 3):
        to = (x + d) % NX
        hid_copies.append(
            go(remote(hid.at[to], hh.at[z, at(x, TOK)], hs_s.at[d - 1], hs_r.at[d - 1], dev(dx=d)))
        )
    hh[z, at(x, TOK)] = hid[x]

    gx_copies = {}
    for d in (2, 1, 3):
        gx_copies[d] = go(
            remote(g, gg.at[at(core, 4), at(y, TOK), at(x, DB)], gx_s.at[d - 1], gx_r.at[d - 1], dev(dx=d))
        )
    load_g.wait()
    gy_copies = {}

    def spread(d):
        src = (x + NX - d) % NX
        piece = gg.at[at(core, 4), at(y, TOK), at(src, DB)]
        for e in (2, 1, 3):
            gy_copies[d, e] = go(remote(piece, piece, gy_s.at[d, e - 1], gy_r.at[d, e - 1], dev(dy=e)))

    spread(0)

    for copy in hid_copies:
        copy.wait_recv()

    def last_hop(way, h):
        return 4 if way == h else 3

    ag_copies = {}

    def ag_send(hop):
        for way in (R, L):
            for h in (way, 1 - way):
                if hop <= last_hop(way, h):
                    b = (z - (hop - 1) + NZ) % NZ if way == R else (z + (hop - 1)) % NZ
                    piece = hh.at[b, h * HALF : (h + 1) * HALF]
                    if hop > 1:
                        ag_copies[way, hop - 1, h].wait_recv()
                    ag_copies[way, hop, h] = go(
                        remote(
                            piece, piece, ag_s.at[way, hop - 1, h], ag_r.at[way, hop - 1, h],
                            dev(dz=1 if way == R else -1),
                        )
                    )

    def turn(b):
        hht[b] = hh[b].T

    ag_send(1)

    w_copies = []
    for d in (2, 1, 3):
        to = (x + d) % NX
        w_copies.append(
            go(remote(w.at[at(to, SUB)], wg.at[:, at(x, DB)], w_s.at[d - 1], w_r.at[d - 1], dev(dx=d)))
        )
    turn(z)

    for d in (1, 3, 2):
        gx_copies[d].wait_recv()
        spread(d)

    ag_send(2)
    turn((z + 1) % NZ)
    turn((z + NZ - 1) % NZ)

    gc_copies = []

    def to_sibling(e):
        rows = gg.at[at(core, 4), at((y + NY - e) % NY, TOK)]
        gc_copies.append(go(remote(rows, rows, gc_s.at[e], gc_r.at[e], dev(dc=1))))

    to_sibling(0)
    for e in (1, 3, 2):
        for d in range(NX):
            gy_copies[d, e].wait_recv()
        to_sibling(e)

    ag_send(3)
    turn((z + 2) % NZ)
    turn((z + NZ - 2) % NZ)

    for copy in gc_copies:
        copy.wait_recv()
    load_w.wait()
    for copy in w_copies:
        copy.wait_recv()

    def multiply(b):
        out = lax.dot_general(gg[b], wg[...], (((1,), (1,)), ((), ())), preferred_element_type=jnp.float32)
        part[b] = out.reshape(NX, TOK, SUB)

    rs_copies = {}

    def rs_send_piece(way, step, h):
        b = (z + 4 - step) % NZ if way == R else (z + 4 + step) % NZ
        value = part[b, :, h * 32 : (h + 1) * 32, :]
        if (way, step - 1, h) in rs_copies:
            rs_copies[way, step - 1, h].wait_recv()
            value = value + rs_recv[way, step - 1, h].astype(jnp.float32)
        rs_send[way, step, h] = value.astype(jnp.bfloat16)
        rs_copies[way, step, h] = go(
            remote(
                rs_send.at[way, step, h], rs_recv.at[way, step, h], rs_s.at[way, step, h], rs_r.at[way, step, h],
                dev(dz=1 if way == R else -1),
            )
        )

    multiply((z + 4) % NZ)
    rs_send_piece(R, 0, 0)
    rs_send_piece(L, 0, 1)

    @pl.loop(0, NZ - 1)
    def _(i):
        multiply((z + 5 + i) % NZ)

    rs_send_piece(R, 1, 1)
    rs_send_piece(L, 1, 0)

    def accumulate(b, first=False):
        @pl.loop(0, NX)
        def _(n):
            cols = at(n, DB)
            out = jnp.dot(hht[b], gg[b, :, cols], preferred_element_type=jnp.float32)
            acc[:, cols] = out if first else acc[:, cols] + out

    accumulate(z, True)

    ag_send(4)
    ag_copies[R, 3, 1].wait_recv()
    ag_copies[L, 3, 0].wait_recv()
    turn((z + 3) % NZ)
    turn((z + NZ - 3) % NZ)

    @pl.loop(0, 3)
    def _(i):
        accumulate((z + 1 + i) % NZ)
        accumulate((z + 7 - i) % NZ)

    ag_copies[R, 4, 0].wait_recv()
    ag_copies[L, 4, 1].wait_recv()
    rs_send_piece(R, 1, 0)
    rs_send_piece(L, 1, 1)
    turn((z + 4) % NZ)
    accumulate((z + 4) % NZ)

    dw_copies = []
    for d in (2, 1, 3):
        to = (x + d) % NX
        dws[to] = acc[:, at(to, DB)].astype(jnp.bfloat16)
        dw_copies.append(go(remote(dws.at[to], dw_out.at[at(x, SUB)], dw_s.at[d - 1], dw_r.at[d - 1], dev(dx=d))))
    dws[x] = acc[:, at(x, DB)].astype(jnp.bfloat16)
    keep_dw = pltpu.make_async_copy(dws.at[x], dw_out.at[at(x, SUB)], lsem.at[4])
    keep_dw.start()

    for step in (2, 3):
        for h in (1, 0):
            rs_send_piece(R, step, h)
            rs_send_piece(L, step, 1 - h)

    f_copies, keep = [], []
    for h in range(2):
        value = part[z, :, h * 32 : (h + 1) * 32, :]
        for way in (R, L):
            rs_copies[way, 3, h].wait_recv()
            value = value + rs_recv[way, 3, h].astype(jnp.float32)
        fin[h] = value.astype(jnp.bfloat16)
        rows = hs_out.at[h * 32 : (h + 1) * 32, pl.ds(pl.multiple_of(x * SUB, 128), SUB)]
        for d in (2, 1, 3):
            to = (x + d) % NX
            f_copies.append(go(remote(fin.at[h, to], rows, f_s.at[h, d - 1], f_r.at[h, d - 1], dev(dx=d))))
        keep.append(pltpu.make_async_copy(fin.at[h, x], rows, lsem.at[5 + h]))
        keep[-1].start()

    keep_dw.wait()
    for copy in keep:
        copy.wait()
    for copy in dw_copies:
        copy.wait_recv()
    for copy in f_copies:
        copy.wait_recv()
    for copy in sent:
        copy.wait_send()


def shards(out_grad, gate_act, up_act, down_weight):
    bf, dma = jnp.bfloat16, pltpu.SemaphoreType.DMA
    anywhere = pl.BlockSpec(memory_space=pl.ANY)
    hidden_grad, grad = pl.pallas_call(
        kernel,
        out_shape=(
            jax.ShapeDtypeStruct((TOK, NX * SUB), bf),
            jax.ShapeDtypeStruct((NX * SUB, DB), bf),
        ),
        in_specs=[anywhere] * 4,
        out_specs=(anywhere, anywhere),
        scratch_shapes=[
            pltpu.VMEM((TOK, NX * SUB), bf),
            pltpu.VMEM((TOK, NX * SUB), bf),
            pltpu.VMEM((NX, TOK, SUB), bf),
            pltpu.VMEM((NZ, BLK, SUB), bf),
            pltpu.VMEM((NZ, SUB, BLK), bf),
            pltpu.VMEM((NZ, BLK, DG), bf),
            pltpu.VMEM((SUB, DG), bf),
            pltpu.VMEM((NZ, NX, TOK, SUB), jnp.float32),
            pltpu.VMEM((2, 4, 2, NX, 32, SUB), bf),
            pltpu.VMEM((2, 4, 2, NX, 32, SUB), bf),
            pltpu.VMEM((2, NX, 32, SUB), bf),
            pltpu.VMEM((SUB, DG), jnp.float32),
            pltpu.VMEM((NX, SUB, DB), bf),
            dma((7,)),
            dma((3,)), dma((3,)),
            dma((3,)), dma((3,)),
            dma((4, 3)), dma((4, 3)),
            dma((4,)), dma((4,)),
            dma((3,)), dma((3,)),
            dma((2, 4, 2)), dma((2, 4, 2)),
            dma((2, 4, 2)), dma((2, 4, 2)),
            dma((2, 3)), dma((2, 3)),
            dma((3,)), dma((3,)),
        ],
        compiler_params=pltpu.CompilerParams(
            collective_id=0, has_side_effects=True, vmem_limit_bytes=52 << 20
        ),
    )(out_grad.reshape(4, TOK, DB), gate_act, up_act, down_weight)
    hidden_grad = hidden_grad.astype(jnp.float32)
    gate_wide = gate_act.astype(jnp.float32)
    up_wide = up_act.astype(jnp.float32)
    sigmoid_gate = jax.nn.sigmoid(gate_wide)
    gate_grad = hidden_grad * up_wide * sigmoid_gate * (1.0 + gate_wide * (1.0 - sigmoid_gate))
    up_grad = hidden_grad * (gate_wide * sigmoid_gate)
    return grad.astype(jnp.float32), gate_grad.astype(jnp.bfloat16), up_grad.astype(jnp.bfloat16)


def solution(mesh):
    in_specs = (P("rows", "cols"), P("cols", "rows"), P("cols", "rows"), P("rows", "cols"))
    out_specs = (P("rows", "cols"), P("cols", "rows"), P("cols", "rows"))
    return jax.shard_map(shards, mesh=mesh, in_specs=in_specs, out_specs=out_specs, check_vma=False)
```

```python
import jax
import jax.numpy as jnp
from jax import lax
from jax.experimental import pallas as pl
from jax.experimental.pallas import tpu as pltpu
from jax.sharding import PartitionSpec as P

MESH = pl.DeviceIdType.MESH
NX, NY, NZ = 4, 4, 8
TOK = 64
SUB = 896
DB = 256
DG = NX * DB
BLK = NX * TOK
Q = 16
NQ = TOK // Q
R, L = 0, 1
F32, BF16 = jnp.float32, jnp.bfloat16


def kernel(
    g, gate, up, w, dw_out, gate_out, up_out,
    gate_v, up_v, hid, hh, gg, wg, part, rs_send, rs_recv, fin, fbuf, gate_f, up_f, acc, dws, land,
    lsem, hs_s, hs_r, gx_s, gx_r, gy_s, gy_r, gc_s, gc_r, w_s, w_r,
    ag_s, ag_r, rs_s, rs_r, f_s, f_r, dw_s, dw_r,
):
    r, c = lax.axis_index("rows"), lax.axis_index("cols")
    y, core, x, z = r // 2, r % 2, c // NZ, c % NZ

    def dev(dx=0, dz=0, dy=0, dc=0):
        return (
            ((y + dy) % NY) * 2 + (core + dc) % 2,
            ((x + dx) % NX) * NZ + (z + dz + NZ) % NZ,
        )

    sent = []

    def send(src, dst, s, d, to):
        copy = pltpu.make_async_remote_copy(
            src_ref=src, dst_ref=dst, send_sem=s, recv_sem=d, device_id=to, device_id_type=MESH
        )
        copy.start()
        sent.append(copy)
        return copy

    def at(i, n):
        return pl.ds(pl.multiple_of(i * n, n), n)

    def lanes(i):
        return pl.ds(pl.multiple_of(i * SUB, 128), SUB)

    peers = [dev(dx=1), dev(dx=2), dev(dx=3), dev(dy=1), dev(dy=2), dev(dy=3), dev(dc=1), dev(dz=1), dev(dz=-1)]
    barrier = pltpu.get_barrier_semaphore()
    for peer in peers:
        pl.semaphore_signal(barrier, inc=1, device_id=peer, device_id_type=MESH)

    load_gate = pltpu.make_async_copy(gate, gate_v, lsem.at[0])
    load_up = pltpu.make_async_copy(up, up_v, lsem.at[1])
    load_g = pltpu.make_async_copy(g, gg.at[at(core, 4), at(y, TOK), at(x, DB)], lsem.at[2])
    load_w = pltpu.make_async_copy(w.at[at(x, SUB)], wg.at[:, at(x, DB)], lsem.at[3])
    load_gate.start()
    load_up.start()
    load_g.start()
    load_w.start()
    load_gate.wait()
    load_up.wait()
    for d in (0, 1, 3, 2):
        to = (x + d) % NX
        wide = gate_v[:, lanes(to)].astype(F32)
        swish = wide * jax.nn.sigmoid(wide)
        value = (swish * up_v[:, lanes(to)].astype(F32)).astype(BF16)
        if d == 0:
            hh[z, at(x, TOK)] = value
        else:
            hid[to] = value
    load_g.wait()
    pl.semaphore_wait(barrier, len(peers))

    ag = {}

    def last_hop(way, d):
        return 4 if (way == R) == (d < 2) else 3

    def gather(hop, d):
        src = (x + NX - d) % NX
        for way in (R, L):
            if hop > 1 and hop - 1 <= last_hop(way, d):
                ag[way, hop - 1, d].wait_recv()
            if hop <= last_hop(way, d):
                b = (z - (hop - 1) + NZ) % NZ if way == R else (z + (hop - 1)) % NZ
                piece = hh.at[b, at(src, TOK)]
                ag[way, hop, d] = send(
                    piece, piece, ag_s.at[way, hop - 1, d], ag_r.at[way, hop - 1, d], dev(dz=1 if way == R else -1)
                )

    gather(1, 0)

    hid_copies = {}
    for d in (1, 3, 2):
        to = (x + d) % NX
        hid_copies[d] = send(hid.at[to], hh.at[z, at(x, TOK)], hs_s.at[d - 1], hs_r.at[d - 1], dev(dx=d))

    gy = {}

    def spread(d):
        src = (x + NX - d) % NX
        piece = gg.at[at(core, 4), at(y, TOK), at(src, DB)]
        for e in (1, 3, 2):
            gy[d, e] = send(piece, piece, gy_s.at[d, e - 1], gy_r.at[d, e - 1], dev(dy=e))

    spread(0)
    for d in (1, 3):
        hid_copies[d].wait_recv()
        gather(1, d)
    gx = {}
    for d in (1, 3, 2):
        gx[d] = send(g, gg.at[at(core, 4), at(y, TOK), at(x, DB)], gx_s.at[d - 1], gx_r.at[d - 1], dev(dx=d))
    hid_copies[2].wait_recv()
    gather(1, 2)
    w_copies = []
    for d in (1, 3, 2):
        to = (x + d) % NX
        w_copies.append(send(w.at[at(to, SUB)], wg.at[:, at(x, DB)], w_s.at[d - 1], w_r.at[d - 1], dev(dx=d)))

    gather(2, 0)
    for d in (1, 3):
        gx[d].wait_recv()
        spread(d)
    gather(2, 1)
    gx[2].wait_recv()
    spread(2)

    gc = []

    def to_sibling(e):
        rows = gg.at[at(core, 4), at((y + NY - e) % NY, TOK)]
        gc.append(send(rows, rows, gc_s.at[e], gc_r.at[e], dev(dc=1)))

    to_sibling(0)
    gather(2, 3)
    gather(2, 2)

    for i in range(NX):
        cols = slice(i * SUB, (i + 1) * SUB)
        wide = gate_v[:, cols].astype(F32)
        sigmoid = jax.nn.sigmoid(wide)
        gate_f[:, cols] = up_v[:, cols].astype(F32) * sigmoid * (1.0 + wide * (1.0 - sigmoid))
        up_f[:, cols] = wide * sigmoid

    for d in (0, 1, 3, 2):
        gather(3, d)
    for e in (1, 3, 2):
        for d in (0, 1, 3, 2):
            gy[d, e].wait_recv()
        to_sibling(e)
    gather(4, 0)
    for copy in gc:
        copy.wait_recv()

    def product(b):
        return lax.dot_general(hh[b], gg[b], (((0,), (0,)), ((), ())), preferred_element_type=F32)

    acc[...] = product(z)

    @pl.loop(0, 2)
    def _(i):
        acc[...] += product((z + 1 + 6 * i) % NZ)

    gather(4, 1)
    load_w.wait()
    for copy in w_copies:
        copy.wait_recv()

    def multiply(b):
        out = lax.dot_general(gg[b], wg[...], (((1,), (1,)), ((), ())), preferred_element_type=F32)
        part[b] = out.reshape(NX, TOK, SUB)

    rs = {}

    def pieces(way, step):
        first, second = ((2, 3), (0, 1)) if way == R else ((0, 1), (2, 3))
        return second if step == 0 else first + second

    def reduce(way, step, k):
        b = (z + 4 - step) % NZ if way == R else (z + 4 + step) % NZ
        value = part[b, :, k * Q : (k + 1) * Q, :]
        if (way, step - 1, k) in rs:
            rs[way, step - 1, k].wait_recv()
            value = value + rs_recv[way, step - 1, k].astype(F32)
        rs_send[way, step, k] = value.astype(BF16)
        rs[way, step, k] = send(
            rs_send.at[way, step, k], rs_recv.at[way, step, k], rs_s.at[way, step, k], rs_r.at[way, step, k],
            dev(dz=1 if way == R else -1),
        )

    def reduce_both(step, ks):
        for i in ks:
            for way in (R, L):
                reduce(way, step, pieces(way, step)[i])

    multiply((z + 4) % NZ)
    reduce_both(0, (0, 1))
    gather(4, 3)
    multiply((z + 3) % NZ)
    multiply((z + 5) % NZ)
    reduce_both(1, (0, 1))
    gather(4, 2)

    @pl.loop(0, 5)
    def _(i):
        multiply((z + 6 + i) % NZ)

    @pl.loop(0, 2)
    def _(i):
        acc[...] += product((z + 2 + 4 * i) % NZ)

    reduce_both(1, (2, 3))

    @pl.loop(0, 2)
    def _(i):
        acc[...] += product((z + 3 + 2 * i) % NZ)

    for way, d in ((R, 0), (R, 1), (L, 3), (L, 2)):
        ag[way, 4, d].wait_recv()
    last = (z + 4) % NZ
    dw = {}
    for d in (1, 3, 2, 0):
        to = (x + d) % NX
        total = acc[:, at(to, DB)] + lax.dot_general(
            hh[last], gg[last, :, at(to, DB)], (((0,), (0,)), ((), ())), preferred_element_type=F32
        )
        if d == 0:
            dw_out[at(x, SUB)] = total
        else:
            dws[to] = total.astype(BF16)
            dw[d] = send(dws.at[to], land.at[x], dw_s.at[d - 1], dw_r.at[d - 1], dev(dx=d))

    reduce_both(2, (0, 1, 2, 3))
    reduce_both(3, (0, 1, 2, 3))
    for d in (1, 3, 2):
        dw[d].wait_recv()
        src = (x + NX - d) % NX
        dw_out[at(src, SUB)] = land[src].astype(F32)

    f = {}
    for k in (2, 0, 3, 1):
        rows = slice(k * Q, (k + 1) * Q)
        value = part[z, :, rows, :]
        for way in (R, L):
            rs[way, 3, k].wait_recv()
            value = value + rs_recv[way, 3, k].astype(F32)
        fin[k] = value.astype(BF16)
        for d in (1, 3, 2):
            to = (x + d) % NX
            f[k, d] = send(fin.at[k, to], fbuf.at[x, rows], f_s.at[k, d - 1], f_r.at[k, d - 1], dev(dx=d))
    for k in (2, 0, 3, 1):
        rows = slice(k * Q, (k + 1) * Q)
        for d in (0, 1, 3, 2):
            src = (x + NX - d) % NX
            if d == 0:
                value = fin[k, x].astype(F32)
            else:
                f[k, d].wait_recv()
                value = fbuf[src, rows].astype(F32)
            gate_out[rows, lanes(src)] = (value * gate_f[rows, lanes(src)]).astype(BF16)
            up_out[rows, lanes(src)] = (value * up_f[rows, lanes(src)]).astype(BF16)

    for copy in sent:
        copy.wait_send()


def copy_out(*refs):
    ins, outs, sems = refs[:3], refs[3:6], refs[6]
    copies = [pltpu.make_async_copy(ins[i], outs[i], sems.at[i]) for i in range(3)]
    for copy in copies:
        copy.start()
    for copy in copies:
        copy.wait()


def shards(out_grad, gate_act, up_act, down_weight):
    dma = pltpu.SemaphoreType.DMA
    anywhere = pl.BlockSpec(memory_space=pl.ANY)
    in_vmem = pl.BlockSpec(memory_space=pltpu.VMEM)
    shapes = [((NX * SUB, DB), F32), ((TOK, NX * SUB), BF16), ((TOK, NX * SUB), BF16)]
    operands = (out_grad.reshape(4, TOK, DB), gate_act, up_act, down_weight)
    results = pl.pallas_call(
        kernel,
        out_shape=[pltpu.VMEM(*shape) for shape in shapes],
        in_specs=[anywhere] * 4,
        out_specs=[in_vmem] * 3,
        scratch_shapes=[
            pltpu.VMEM((TOK, NX * SUB), BF16),
            pltpu.VMEM((TOK, NX * SUB), BF16),
            pltpu.VMEM((NX, TOK, SUB), BF16),
            pltpu.VMEM((NZ, BLK, SUB), BF16),
            pltpu.VMEM((NZ, BLK, DG), BF16),
            pltpu.VMEM((SUB, DG), BF16),
            pltpu.VMEM((NZ, NX, TOK, SUB), F32),
            pltpu.VMEM((2, 4, NQ, NX, Q, SUB), BF16),
            pltpu.VMEM((2, 4, NQ, NX, Q, SUB), BF16),
            pltpu.VMEM((NQ, NX, Q, SUB), BF16),
            pltpu.VMEM((NX, TOK, SUB), BF16),
            pltpu.VMEM((TOK, NX * SUB), F32),
            pltpu.VMEM((TOK, NX * SUB), F32),
            pltpu.VMEM((SUB, DG), F32),
            pltpu.VMEM((NX, SUB, DB), BF16),
            pltpu.VMEM((NX, SUB, DB), BF16),
            dma((4,)),
            dma((3,)), dma((3,)),
            dma((3,)), dma((3,)),
            dma((4, 3)), dma((4, 3)),
            dma((4,)), dma((4,)),
            dma((3,)), dma((3,)),
            dma((2, 4, 4)), dma((2, 4, 4)),
            dma((2, 4, NQ)), dma((2, 4, NQ)),
            dma((NQ, 3)), dma((NQ, 3)),
            dma((3,)), dma((3,)),
        ],
        compiler_params=pltpu.CompilerParams(
            collective_id=0, has_side_effects=True, vmem_limit_bytes=50 << 20
        ),
    )(*[pltpu.with_memory_space_constraint(operand, pltpu.HBM) for operand in operands])
    return pl.pallas_call(
        copy_out,
        out_shape=[jax.ShapeDtypeStruct(*shape) for shape in shapes],
        in_specs=[anywhere] * 3,
        out_specs=[anywhere] * 3,
        scratch_shapes=[dma((3,))],
        compiler_params=pltpu.CompilerParams(vmem_limit_bytes=1 << 20),
    )(*[pltpu.with_memory_space_constraint(result, pltpu.VMEM) for result in results])


def solution(mesh):
    in_specs = (P("rows", "cols"), P("cols", "rows"), P("cols", "rows"), P("rows", "cols"))
    out_specs = (P("rows", "cols"), P("cols", "rows"), P("cols", "rows"))
    return jax.shard_map(shards, mesh=mesh, in_specs=in_specs, out_specs=out_specs, check_vma=False)
```

```python
import jax
import jax.numpy as jnp
from jax import lax
from jax.experimental import pallas as pl
from jax.experimental.pallas import tpu as pltpu
from jax.sharding import PartitionSpec as P

MESH = pl.DeviceIdType.MESH
NX, NY, NZ = 4, 4, 8
TOK = 64
SUB = 896
DB = 256
DG = NX * DB
BLK = NX * TOK
Q = 16
NQ = TOK // Q
R, L = 0, 1
F32, BF16 = jnp.float32, jnp.bfloat16


def kernel(
    g, gate, up, w, dw_out, gate_out, up_out,
    gate_v, up_v, hid, hh, gg, wg, part, rs_send, rs_recv, fin, fbuf, gate_f, up_f, acc, dws, land, x_land,
    act_sem, lsem, hs_s, hs_r, gx_s, gx_r, gy_s, gy_r, gc_s, gc_r, w_s, w_r,
    ag_s, ag_r, rs_s, rs_r, f_s, f_r, x_s, x_r, dw_s, dw_r,
):
    r, c = lax.axis_index("rows"), lax.axis_index("cols")
    y, core, x, z = r // 2, r % 2, c // NZ, c % NZ

    def dev(dx=0, dz=0, dy=0, dc=0):
        return (
            ((y + dy) % NY) * 2 + (core + dc) % 2,
            ((x + dx) % NX) * NZ + (z + dz + NZ) % NZ,
        )

    sent = []

    def send(src, dst, s, d, to):
        copy = pltpu.make_async_remote_copy(
            src_ref=src, dst_ref=dst, send_sem=s, recv_sem=d, device_id=to, device_id_type=MESH
        )
        copy.start()
        sent.append(copy)
        return copy

    def drain(count):
        for copy in sent[:count]:
            copy.wait_send()
        del sent[:count]

    def at(i, n):
        return pl.ds(pl.multiple_of(i * n, n), n)

    def lanes(i):
        return pl.ds(pl.multiple_of(i * SUB, 128), SUB)

    peers = [dev(dx=1), dev(dx=2), dev(dx=3), dev(dy=1), dev(dy=2), dev(dy=3), dev(dc=1), dev(dz=1), dev(dz=-1)]
    barrier = pltpu.get_barrier_semaphore()
    for peer in peers:
        pl.semaphore_signal(barrier, inc=1, device_id=peer, device_id_type=MESH)

    loads = {}
    for d in (0, 1, 3, 2):
        cols = lanes((x + d) % NX)
        for i, (src, dst) in enumerate(((gate, gate_v), (up, up_v))):
            loads[d, i] = pltpu.make_async_copy(src.at[:, cols], dst.at[:, cols], act_sem.at[d, i])
            loads[d, i].start()
    load_g = pltpu.make_async_copy(g, gg.at[at(core, 4), at(y, TOK), at(x, DB)], lsem.at[0])
    load_w = pltpu.make_async_copy(w.at[at(x, SUB)], wg.at[:, at(x, DB)], lsem.at[1])
    load_g.start()
    load_w.start()

    def hidden(d):
        loads[d, 0].wait()
        loads[d, 1].wait()
        cols = lanes((x + d) % NX)
        wide = gate_v[:, cols].astype(F32)
        swish = wide * jax.nn.sigmoid(wide)
        return (swish * up_v[:, cols].astype(F32)).astype(BF16)

    hh[z, at(x, TOK)] = hidden(0)
    pl.semaphore_wait(barrier, len(peers))

    ag = {}

    def last_hop(way, d):
        return 4 if (way == R) == (d < 2) else 3

    def gather(hop, d):
        src = (x + NX - d) % NX
        for way in (R, L):
            if hop > 1 and hop - 1 <= last_hop(way, d):
                ag[way, hop - 1, d].wait_recv()
            if hop <= last_hop(way, d):
                b = (z - (hop - 1) + NZ) % NZ if way == R else (z + (hop - 1)) % NZ
                piece = hh.at[b, at(src, TOK)]
                ag[way, hop, d] = send(
                    piece, piece, ag_s.at[way, hop - 1, d], ag_r.at[way, hop - 1, d], dev(dz=1 if way == R else -1)
                )

    gather(1, 0)

    hid_copies = {}
    for d in (1, 3, 2):
        to = (x + d) % NX
        hid[to] = hidden(d)
        hid_copies[d] = send(hid.at[to], hh.at[z, at(x, TOK)], hs_s.at[d - 1], hs_r.at[d - 1], dev(dx=d))

    gy, gc = {}, []

    def rows_of(d, e, first=0, n=4):
        src = (x + NX - d) % NX
        return gg.at[pl.ds(core * 4 + first, n), at((y + NY - e) % NY, TOK), at(src, DB)]

    def to_sibling(d, i, piece):
        gc.append(send(piece, piece, gc_s.at[d, i], gc_r.at[d, i], dev(dc=1)))

    def spread(d):
        piece = rows_of(d, 0)
        for i, e in enumerate((1, 3)):
            gy[d, i] = send(piece, piece, gy_s.at[d, i], gy_r.at[d, i], dev(dy=e))
        to_sibling(d, 4, piece)

    def relay(d):
        for i, e in enumerate((1, 3)):
            gy[d, i].wait_recv()
            half = rows_of(d, e, 2 * i, 2)
            gy[d, 2 + i] = send(half, half, gy_s.at[d, 2 + i], gy_r.at[d, 2 + i], dev(dy=e))
            to_sibling(d, i, rows_of(d, e))

    def finish(d):
        for i in range(2):
            gy[d, 2 + i].wait_recv()
            to_sibling(d, 2 + i, rows_of(d, 2, 2 * i, 2))

    load_g.wait()
    spread(0)
    for d in (1, 3):
        hid_copies[d].wait_recv()
        gather(1, d)
    gx = {}
    for d in (1, 3, 2):
        gx[d] = send(g, gg.at[at(core, 4), at(y, TOK), at(x, DB)], gx_s.at[d - 1], gx_r.at[d - 1], dev(dx=d))
    hid_copies[2].wait_recv()
    gather(1, 2)
    w_copies = []
    for d in (1, 3, 2):
        to = (x + d) % NX
        w_copies.append(send(w.at[at(to, SUB)], wg.at[:, at(x, DB)], w_s.at[d - 1], w_r.at[d - 1], dev(dx=d)))
    gather(2, 0)
    relay(0)
    gather(2, 1)
    for d in (1, 3):
        gx[d].wait_recv()
        spread(d)
    gather(2, 3)
    gx[2].wait_recv()
    spread(2)
    gather(2, 2)

    for i in range(NX):
        cols = slice(i * SUB, (i + 1) * SUB)
        wide = gate_v[:, cols].astype(F32)
        sigmoid = jax.nn.sigmoid(wide)
        gate_f[:, cols] = up_v[:, cols].astype(F32) * sigmoid * (1.0 + wide * (1.0 - sigmoid))
        up_f[:, cols] = wide * sigmoid

    relay(1)
    gather(3, 0)
    relay(3)
    finish(0)
    gather(3, 1)
    relay(2)
    finish(1)
    gather(3, 3)
    finish(3)
    gather(3, 2)
    finish(2)
    for copy in gc:
        copy.wait_recv()

    def product(b):
        return lax.dot_general(hh[b], gg[b], (((0,), (0,)), ((), ())), preferred_element_type=F32)

    acc[...] = product(z)

    @pl.loop(0, 2)
    def _(i):
        acc[...] += product((z + 1 + 6 * i) % NZ)

    gather(4, 0)

    @pl.loop(0, 2)
    def _(i):
        acc[...] += product((z + 2 + 4 * i) % NZ)

    gather(4, 1)
    gather(4, 3)
    gather(4, 2)

    @pl.loop(0, 2)
    def _(i):
        acc[...] += product((z + 3 + 2 * i) % NZ)

    load_w.wait()
    for copy in w_copies:
        copy.wait_recv()

    def multiply(b):
        out = lax.dot_general(gg[b], wg[...], (((1,), (1,)), ((), ())), preferred_element_type=F32)
        part[b] = out.reshape(NX, TOK, SUB)

    rs = {}

    order = {
        R: ((1, 0), (3, 2, 1, 0), (3, 1, 2, 0), (2, 0)),
        L: ((3, 2), (1, 0, 3, 2), (1, 3, 0, 2), (0, 2)),
    }

    def running(way, step, k):
        b = (z + 4 - step) % NZ if way == R else (z + 4 + step) % NZ
        value = part[b, :, k * Q : (k + 1) * Q, :]
        if (way, step - 1, k) in rs:
            rs[way, step - 1, k].wait_recv()
            value = value + rs_recv[way, step - 1, k].astype(F32)
        return value.astype(BF16)

    def pass_on(way, step, k, src):
        rs[way, step, k] = send(
            src, rs_recv.at[way, step, k], rs_s.at[way, step, k], rs_r.at[way, step, k], dev(dz=1 if way == R else -1)
        )

    def reduce_both(step, places):
        for i in places:
            for way in (R, L):
                k = order[way][step][i]
                rs_send[way, step, k] = running(way, step, k)
                pass_on(way, step, k, rs_send.at[way, step, k])

    early = (3, 1)
    swapped = {}

    def swap(who, k, src):
        i = early.index(k)
        for d in (1, 3, 2):
            swapped[who, k, d] = send(
                src.at[(x + d) % NX], x_land.at[who, i, x], x_s.at[who, i, d - 1], x_r.at[who, i, d - 1], dev(dx=d)
            )
        x_land[who, i, x] = src[x]

    def wait_swap(who, k):
        for d in (1, 3, 2):
            swapped[who, k, d].wait_recv()

    multiply((z + 4) % NZ)
    reduce_both(0, (0, 1))
    multiply((z + 3) % NZ)
    multiply((z + 5) % NZ)
    reduce_both(1, (0, 1))

    @pl.loop(0, 5)
    def _(i):
        multiply((z + 6 + i) % NZ)

    for way, d in ((R, 0), (R, 1), (L, 3), (L, 2)):
        ag[way, 4, d].wait_recv()
    last = (z + 4) % NZ
    dw = {}
    for d in (1, 3, 2, 0):
        to = (x + d) % NX
        total = acc[:, at(to, DB)] + lax.dot_general(
            hh[last], gg[last, :, at(to, DB)], (((0,), (0,)), ((), ())), preferred_element_type=F32
        )
        if d == 0:
            dw_out[at(x, SUB)] = total
        else:
            dws[to] = total.astype(BF16)
            dw[d] = send(dws.at[to], land.at[x], dw_s.at[d - 1], dw_r.at[d - 1], dev(dx=d))

    before = len(sent) - 11
    reduce_both(1, (2, 3))
    drain(before)
    before = len(sent)
    reduce_both(2, (0, 1, 2, 3))
    drain(before)
    before = len(sent)
    for way, k in ((R, 3), (L, 1), (R, 1), (L, 3)):
        rs_send[way, 3, k] = running(way, 3, k)
        swap(way, k, rs_send.at[way, 3, k])
    for k in early:
        fin[k] = part[z, :, k * Q : (k + 1) * Q, :].astype(BF16)
        swap(2, k, fin.at[k])
    reduce_both(3, (0, 1))
    for k in early:
        for way in (R, L):
            wait_swap(way, k)
            pass_on(way, 3, k, x_land.at[way, early.index(k)])
    drain(before)
    for d in (1, 3, 2):
        dw[d].wait_recv()
        src = (x + NX - d) % NX
        dw_out[at(src, SUB)] = land[src].astype(F32)

    f = {}
    for i, k in enumerate((2, 0)):
        rows = slice(k * Q, (k + 1) * Q)
        value = part[z, :, rows, :]
        for way in (R, L):
            rs[way, 3, k].wait_recv()
            value = value + rs_recv[way, 3, k].astype(F32)
        fin[k] = value.astype(BF16)
        for d in (1, 3, 2):
            to = (x + d) % NX
            f[k, d] = send(fin.at[k, to], fbuf.at[i, x], f_s.at[i, d - 1], f_r.at[i, d - 1], dev(dx=d))
        fbuf[i, x] = fin[k, x]

    def result(k, src, value):
        rows, cols = slice(k * Q, (k + 1) * Q), slice(src * SUB, (src + 1) * SUB)
        gate_out[rows, cols] = (value * gate_f[rows, cols]).astype(BF16)
        up_out[rows, cols] = (value * up_f[rows, cols]).astype(BF16)

    for i, k in enumerate((2, 0)):
        for d in (1, 3, 2):
            f[k, d].wait_recv()
        for src in range(NX):
            result(k, src, fbuf[i, src].astype(F32))
    for i, k in enumerate(early):
        wait_swap(2, k)
        for way in (R, L):
            rs[way, 3, k].wait_recv()
        for src in range(NX):
            value = x_land[2, i, src].astype(F32)
            for way in (R, L):
                value = value + rs_recv[way, 3, k, src].astype(F32)
            result(k, src, value)

    drain(len(sent))


def copy_out(*refs):
    ins, outs, sems = refs[:3], refs[3:6], refs[6]
    copies = [pltpu.make_async_copy(ins[i], outs[i], sems.at[i]) for i in range(3)]
    for copy in copies:
        copy.start()
    for copy in copies:
        copy.wait()


def shards(out_grad, gate_act, up_act, down_weight):
    dma = pltpu.SemaphoreType.DMA
    anywhere = pl.BlockSpec(memory_space=pl.ANY)
    in_vmem = pl.BlockSpec(memory_space=pltpu.VMEM)
    shapes = [((NX * SUB, DB), F32), ((TOK, NX * SUB), BF16), ((TOK, NX * SUB), BF16)]
    operands = (out_grad.reshape(4, TOK, DB), gate_act, up_act, down_weight)
    results = pl.pallas_call(
        kernel,
        out_shape=[pltpu.VMEM(*shape) for shape in shapes],
        in_specs=[anywhere] * 4,
        out_specs=[in_vmem] * 3,
        scratch_shapes=[
            pltpu.VMEM((TOK, NX * SUB), BF16),
            pltpu.VMEM((TOK, NX * SUB), BF16),
            pltpu.VMEM((NX, TOK, SUB), BF16),
            pltpu.VMEM((NZ, BLK, SUB), BF16),
            pltpu.VMEM((NZ, BLK, DG), BF16),
            pltpu.VMEM((SUB, DG), BF16),
            pltpu.VMEM((NZ, NX, TOK, SUB), F32),
            pltpu.VMEM((2, 4, NQ, NX, Q, SUB), BF16),
            pltpu.VMEM((2, 4, NQ, NX, Q, SUB), BF16),
            pltpu.VMEM((NQ, NX, Q, SUB), BF16),
            pltpu.VMEM((2, NX, Q, SUB), BF16),
            pltpu.VMEM((TOK, NX * SUB), F32),
            pltpu.VMEM((TOK, NX * SUB), F32),
            pltpu.VMEM((SUB, DG), F32),
            pltpu.VMEM((NX, SUB, DB), BF16),
            pltpu.VMEM((NX, SUB, DB), BF16),
            pltpu.VMEM((3, 2, NX, Q, SUB), BF16),
            dma((4, 2)), dma((2,)),
            dma((3,)), dma((3,)),
            dma((3,)), dma((3,)),
            dma((4, 4)), dma((4, 4)),
            dma((4, 5)), dma((4, 5)),
            dma((3,)), dma((3,)),
            dma((2, 4, 4)), dma((2, 4, 4)),
            dma((2, 4, NQ)), dma((2, 4, NQ)),
            dma((2, 3)), dma((2, 3)),
            dma((3, 2, 3)), dma((3, 2, 3)),
            dma((3,)), dma((3,)),
        ],
        compiler_params=pltpu.CompilerParams(
            collective_id=0, has_side_effects=True, vmem_limit_bytes=50 << 20
        ),
    )(*[pltpu.with_memory_space_constraint(operand, pltpu.HBM) for operand in operands])
    return pl.pallas_call(
        copy_out,
        out_shape=[jax.ShapeDtypeStruct(*shape) for shape in shapes],
        in_specs=[anywhere] * 3,
        out_specs=[anywhere] * 3,
        scratch_shapes=[dma((3,))],
        compiler_params=pltpu.CompilerParams(vmem_limit_bytes=1 << 20),
    )(*[pltpu.with_memory_space_constraint(result, pltpu.VMEM) for result in results])


def solution(mesh):
    in_specs = (P("rows", "cols"), P("cols", "rows"), P("cols", "rows"), P("rows", "cols"))
    out_specs = (P("rows", "cols"), P("cols", "rows"), P("cols", "rows"))
    return jax.shard_map(shards, mesh=mesh, in_specs=in_specs, out_specs=out_specs, check_vma=False)
```

```python
import jax
import jax.numpy as jnp
from jax import lax
from jax.experimental import pallas as pl
from jax.experimental.pallas import tpu as pltpu
from jax.sharding import PartitionSpec as P

MESH = pl.DeviceIdType.MESH
NX, NY, NZ = 4, 4, 8
TOK = 64
SUB = 896
DB = 256
DG = NX * DB
BLK = NX * TOK
Q = 16
NQ = TOK // Q
OWN = 2
R, L = 0, 1
F32, BF16 = jnp.float32, jnp.bfloat16


def kernel(
    g, gate, up, w, dw_out, gate_out, up_out,
    gate_v, up_v, hid, hh, gg, wg, part, rs_send, rs_recv, fin, fbuf, gate_f, up_f, acc, dws, land, x_land,
    act_sem, lsem, hs_s, hs_r, gx_s, gx_r, gy_s, gy_r, gc_s, gc_r, w_s, w_r,
    ag_s, ag_r, rs_s, rs_r, f_s, f_r, x_s, x_r, dw_s, dw_r,
):
    r, c = lax.axis_index("rows"), lax.axis_index("cols")
    y, core, x, z = r // 2, r % 2, c // NZ, c % NZ

    def dev(dx=0, dz=0, dy=0, dc=0):
        return (
            ((y + dy) % NY) * 2 + (core + dc) % 2,
            ((x + dx) % NX) * NZ + (z + dz + NZ) % NZ,
        )

    sent = []

    def send(src, dst, s, d, to):
        copy = pltpu.make_async_remote_copy(
            src_ref=src, dst_ref=dst, send_sem=s, recv_sem=d, device_id=to, device_id_type=MESH
        )
        copy.start()
        sent.append(copy)
        return copy

    def drain(count):
        for copy in sent[:count]:
            copy.wait_send()
        del sent[:count]

    def at(i, n):
        return pl.ds(pl.multiple_of(i * n, n), n)

    def lanes(i):
        return pl.ds(pl.multiple_of(i * SUB, 128), SUB)

    peers = [dev(dx=1), dev(dx=2), dev(dx=3), dev(dy=1), dev(dy=2), dev(dy=3), dev(dc=1), dev(dz=1), dev(dz=-1)]
    barrier = pltpu.get_barrier_semaphore()
    for peer in peers:
        pl.semaphore_signal(barrier, inc=1, device_id=peer, device_id_type=MESH)

    loads = {}
    for d in (0, 1, 3, 2):
        cols = lanes((x + d) % NX)
        for i, (src, dst) in enumerate(((gate, gate_v), (up, up_v))):
            loads[d, i] = pltpu.make_async_copy(src.at[:, cols], dst.at[:, cols], act_sem.at[d, i])
            loads[d, i].start()
    load_g = pltpu.make_async_copy(g, gg.at[at(core, 4), at(y, TOK), at(x, DB)], lsem.at[0])
    load_w = pltpu.make_async_copy(w.at[at(x, SUB)], wg.at[:, at(x, DB)], lsem.at[1])
    load_g.start()
    load_w.start()

    def hidden(d):
        loads[d, 0].wait()
        loads[d, 1].wait()
        cols = lanes((x + d) % NX)
        wide = gate_v[:, cols].astype(F32)
        swish = wide * jax.nn.sigmoid(wide)
        return (swish * up_v[:, cols].astype(F32)).astype(BF16)

    hh[z, at(x, TOK)] = hidden(0)
    pl.semaphore_wait(barrier, len(peers))

    ag = {}

    def last_hop(way, d):
        return 4 if (way == R) == (d < 2) else 3

    def gather(hop, d):
        src = (x + NX - d) % NX
        parts = OWN if d == 0 else 1
        n = TOK // parts
        for way in (R, L):
            for i in range(parts):
                j = i if d == 0 else OWN + d - 1
                if hop > 1 and hop - 1 <= last_hop(way, d):
                    ag[way, hop - 1, j].wait_recv()
                if hop <= last_hop(way, d):
                    b = (z - (hop - 1) + NZ) % NZ if way == R else (z + (hop - 1)) % NZ
                    piece = hh.at[b, pl.ds(pl.multiple_of(src * TOK + i * n, n), n)]
                    ag[way, hop, j] = send(
                        piece, piece, ag_s.at[way, hop - 1, j], ag_r.at[way, hop - 1, j], dev(dz=1 if way == R else -1)
                    )

    gather(1, 0)

    hid_copies = {}
    for d in (1, 3, 2):
        to = (x + d) % NX
        hid[to] = hidden(d)
        hid_copies[d] = send(hid.at[to], hh.at[z, at(x, TOK)], hs_s.at[d - 1], hs_r.at[d - 1], dev(dx=d))

    gy, gc = {}, []

    def rows_of(d, e, first=0, n=4):
        src = (x + NX - d) % NX
        return gg.at[pl.ds(core * 4 + first, n), at((y + NY - e) % NY, TOK), at(src, DB)]

    def to_sibling(d, i, piece):
        gc.append(send(piece, piece, gc_s.at[d, i], gc_r.at[d, i], dev(dc=1)))

    def spread(d):
        piece = rows_of(d, 0)
        for i, e in enumerate((1, 3)):
            gy[d, i] = send(piece, piece, gy_s.at[d, i], gy_r.at[d, i], dev(dy=e))
        to_sibling(d, 4, piece)

    def relay(d):
        for i, e in enumerate((1, 3)):
            gy[d, i].wait_recv()
            half = rows_of(d, e, 2 * i, 2)
            gy[d, 2 + i] = send(half, half, gy_s.at[d, 2 + i], gy_r.at[d, 2 + i], dev(dy=e))
            to_sibling(d, i, rows_of(d, e))

    def finish(d):
        for i in range(2):
            gy[d, 2 + i].wait_recv()
            to_sibling(d, 2 + i, rows_of(d, 2, 2 * i, 2))

    load_g.wait()
    spread(0)
    gather(2, 0)
    for d in (1, 3):
        hid_copies[d].wait_recv()
        gather(1, d)
    gx = {}
    for d in (1, 3, 2):
        gx[d] = send(g, gg.at[at(core, 4), at(y, TOK), at(x, DB)], gx_s.at[d - 1], gx_r.at[d - 1], dev(dx=d))
    hid_copies[2].wait_recv()
    gather(1, 2)
    w_copies = []
    for d in (1, 3, 2):
        to = (x + d) % NX
        w_copies.append(send(w.at[at(to, SUB)], wg.at[:, at(x, DB)], w_s.at[d - 1], w_r.at[d - 1], dev(dx=d)))
    relay(0)
    gather(2, 1)
    for d in (1, 3):
        gx[d].wait_recv()
        spread(d)
    gather(2, 3)
    gx[2].wait_recv()
    spread(2)
    gather(2, 2)

    for i in range(NX):
        cols = slice(i * SUB, (i + 1) * SUB)
        wide = gate_v[:, cols].astype(F32)
        sigmoid = jax.nn.sigmoid(wide)
        gate_f[:, cols] = up_v[:, cols].astype(F32) * sigmoid * (1.0 + wide * (1.0 - sigmoid))
        up_f[:, cols] = wide * sigmoid

    relay(1)
    gather(3, 0)
    relay(3)
    finish(0)
    gather(3, 1)
    relay(2)
    finish(1)
    gather(3, 3)
    finish(3)
    gather(3, 2)
    finish(2)
    for copy in gc:
        copy.wait_recv()

    def product(b):
        return lax.dot_general(hh[b], gg[b], (((0,), (0,)), ((), ())), preferred_element_type=F32)

    acc[...] = product(z)

    @pl.loop(0, 2)
    def _(i):
        acc[...] += product((z + 1 + 6 * i) % NZ)

    gather(4, 0)

    @pl.loop(0, 2)
    def _(i):
        acc[...] += product((z + 2 + 4 * i) % NZ)

    gather(4, 1)
    gather(4, 3)
    gather(4, 2)

    @pl.loop(0, 2)
    def _(i):
        acc[...] += product((z + 3 + 2 * i) % NZ)

    load_w.wait()
    for copy in w_copies:
        copy.wait_recv()

    def multiply(b):
        out = lax.dot_general(gg[b], wg[...], (((1,), (1,)), ((), ())), preferred_element_type=F32)
        part[b] = out.reshape(NX, TOK, SUB)

    rs = {}

    order = {
        R: ((1, 0), (3, 2, 1, 0), (3, 2, 0, 1), (2, 0)),
        L: ((2, 3), (1, 0, 2, 3), (1, 2, 0, 3), (2, 0)),
    }

    def running(way, step, k):
        b = (z + 4 - step) % NZ if way == R else (z + 4 + step) % NZ
        value = part[b, :, k * Q : (k + 1) * Q, :]
        if (way, step - 1, k) in rs:
            rs[way, step - 1, k].wait_recv()
            value = value + rs_recv[way, step - 1, k].astype(F32)
        return value.astype(BF16)

    def pass_on(way, step, k, src):
        rs[way, step, k] = send(
            src, rs_recv.at[way, step, k], rs_s.at[way, step, k], rs_r.at[way, step, k], dev(dz=1 if way == R else -1)
        )

    def reduce_both(step, places):
        for i in places:
            for way in (R, L):
                k = order[way][step][i]
                rs_send[way, step, k] = running(way, step, k)
                pass_on(way, step, k, rs_send.at[way, step, k])

    early, home = (3, 1), (2, 0)
    swapped = {}

    def swap(who, k, src):
        i = early.index(k)
        for d in (1, 3, 2):
            swapped[who, k, d] = send(
                src.at[(x + d) % NX], x_land.at[who, i, x], x_s.at[who, i, d - 1], x_r.at[who, i, d - 1], dev(dx=d)
            )
        x_land[who, i, x] = src[x]

    def wait_swap(who, k):
        for d in (1, 3, 2):
            swapped[who, k, d].wait_recv()

    multiply((z + 4) % NZ)
    reduce_both(0, (0, 1))
    multiply((z + 3) % NZ)
    multiply((z + 5) % NZ)
    reduce_both(1, (0, 1))

    @pl.loop(0, 5)
    def _(i):
        multiply((z + 6 + i) % NZ)

    for way, js in ((R, range(OWN + 1)), (L, (OWN + 2, OWN + 1))):
        for j in js:
            ag[way, 4, j].wait_recv()
    last = (z + 4) % NZ
    dw = {}
    for d in (1, 3, 2, 0):
        to = (x + d) % NX
        total = acc[:, at(to, DB)] + lax.dot_general(
            hh[last], gg[last, :, at(to, DB)], (((0,), (0,)), ((), ())), preferred_element_type=F32
        )
        if d == 0:
            dw_out[at(x, SUB)] = total
        else:
            dws[to] = total.astype(BF16)
            dw[d] = send(dws.at[to], land.at[x], dw_s.at[d - 1], dw_r.at[d - 1], dev(dx=d))

    before = len(sent) - 11
    reduce_both(1, (2, 3))
    drain(before)
    before = len(sent)
    reduce_both(2, (0, 1, 2, 3))
    drain(before)
    before = len(sent)
    def swap_running(pairs):
        for way, k in pairs:
            rs_send[way, 3, k] = running(way, 3, k)
            swap(way, k, rs_send.at[way, 3, k])

    swap_running(((R, 3), (L, 1)))
    reduce_both(3, (0, 1))
    swap_running(((R, 1), (L, 3)))
    for k in early:
        fin[k] = part[z, :, k * Q : (k + 1) * Q, :].astype(BF16)
        swap(2, k, fin.at[k])

    f = {}

    def give_back(k):
        i = home.index(k)
        value = part[z, :, k * Q : (k + 1) * Q, :]
        for way in (R, L):
            rs[way, 3, k].wait_recv()
            value = value + rs_recv[way, 3, k].astype(F32)
        fin[k] = value.astype(BF16)
        for d in (1, 3, 2):
            to = (x + d) % NX
            f[k, d] = send(fin.at[k, to], fbuf.at[i, x], f_s.at[i, d - 1], f_r.at[i, d - 1], dev(dx=d))
        fbuf[i, x] = fin[k, x]

    def last_step(pairs):
        for way, k in pairs:
            wait_swap(way, k)
            pass_on(way, 3, k, x_land.at[way, early.index(k)])

    last_step(((R, 3), (L, 1)))
    give_back(home[0])
    last_step(((R, 1), (L, 3)))
    give_back(home[1])
    drain(before)
    for d in (1, 3, 2):
        dw[d].wait_recv()
        src = (x + NX - d) % NX
        dw_out[at(src, SUB)] = land[src].astype(F32)

    def result(k, src, value):
        rows, cols = slice(k * Q, (k + 1) * Q), slice(src * SUB, (src + 1) * SUB)
        gate_out[rows, cols] = (value * gate_f[rows, cols]).astype(BF16)
        up_out[rows, cols] = (value * up_f[rows, cols]).astype(BF16)

    for i, k in enumerate(home):
        for d in (1, 3, 2):
            f[k, d].wait_recv()
        for src in range(NX):
            result(k, src, fbuf[i, src].astype(F32))
    for i, k in enumerate(early):
        wait_swap(2, k)
        for way in (R, L):
            rs[way, 3, k].wait_recv()
        for src in range(NX):
            value = x_land[2, i, src].astype(F32)
            for way in (R, L):
                value = value + rs_recv[way, 3, k, src].astype(F32)
            result(k, src, value)

    drain(len(sent))


def copy_out(*refs):
    ins, outs, sems = refs[:3], refs[3:6], refs[6]
    copies = [pltpu.make_async_copy(ins[i], outs[i], sems.at[i]) for i in range(3)]
    for copy in copies:
        copy.start()
    for copy in copies:
        copy.wait()


def shards(out_grad, gate_act, up_act, down_weight):
    dma = pltpu.SemaphoreType.DMA
    anywhere = pl.BlockSpec(memory_space=pl.ANY)
    in_vmem = pl.BlockSpec(memory_space=pltpu.VMEM)
    shapes = [((NX * SUB, DB), F32), ((TOK, NX * SUB), BF16), ((TOK, NX * SUB), BF16)]
    operands = (out_grad.reshape(4, TOK, DB), gate_act, up_act, down_weight)
    results = pl.pallas_call(
        kernel,
        out_shape=[pltpu.VMEM(*shape) for shape in shapes],
        in_specs=[anywhere] * 4,
        out_specs=[in_vmem] * 3,
        scratch_shapes=[
            pltpu.VMEM((TOK, NX * SUB), BF16),
            pltpu.VMEM((TOK, NX * SUB), BF16),
            pltpu.VMEM((NX, TOK, SUB), BF16),
            pltpu.VMEM((NZ, BLK, SUB), BF16),
            pltpu.VMEM((NZ, BLK, DG), BF16),
            pltpu.VMEM((SUB, DG), BF16),
            pltpu.VMEM((NZ, NX, TOK, SUB), F32),
            pltpu.VMEM((2, 4, NQ, NX, Q, SUB), BF16),
            pltpu.VMEM((2, 4, NQ, NX, Q, SUB), BF16),
            pltpu.VMEM((NQ, NX, Q, SUB), BF16),
            pltpu.VMEM((2, NX, Q, SUB), BF16),
            pltpu.VMEM((TOK, NX * SUB), F32),
            pltpu.VMEM((TOK, NX * SUB), F32),
            pltpu.VMEM((SUB, DG), F32),
            pltpu.VMEM((NX, SUB, DB), BF16),
            pltpu.VMEM((NX, SUB, DB), BF16),
            pltpu.VMEM((3, 2, NX, Q, SUB), BF16),
            dma((4, 2)), dma((2,)),
            dma((3,)), dma((3,)),
            dma((3,)), dma((3,)),
            dma((4, 4)), dma((4, 4)),
            dma((4, 5)), dma((4, 5)),
            dma((3,)), dma((3,)),
            dma((2, 4, OWN + 3)), dma((2, 4, OWN + 3)),
            dma((2, 4, NQ)), dma((2, 4, NQ)),
            dma((2, 3)), dma((2, 3)),
            dma((3, 2, 3)), dma((3, 2, 3)),
            dma((3,)), dma((3,)),
        ],
        compiler_params=pltpu.CompilerParams(
            collective_id=0, has_side_effects=True, vmem_limit_bytes=50 << 20
        ),
    )(*[pltpu.with_memory_space_constraint(operand, pltpu.HBM) for operand in operands])
    return pl.pallas_call(
        copy_out,
        out_shape=[jax.ShapeDtypeStruct(*shape) for shape in shapes],
        in_specs=[anywhere] * 3,
        out_specs=[anywhere] * 3,
        scratch_shapes=[dma((3,))],
        compiler_params=pltpu.CompilerParams(vmem_limit_bytes=1 << 20),
    )(*[pltpu.with_memory_space_constraint(result, pltpu.VMEM) for result in results])


def solution(mesh):
    in_specs = (P("rows", "cols"), P("cols", "rows"), P("cols", "rows"), P("rows", "cols"))
    out_specs = (P("rows", "cols"), P("cols", "rows"), P("cols", "rows"))
    return jax.shard_map(shards, mesh=mesh, in_specs=in_specs, out_specs=out_specs, check_vma=False)
```

```python
import jax
import jax.numpy as jnp
from jax import lax
from jax.experimental import pallas as pl
from jax.experimental.pallas import tpu as pltpu
from jax.sharding import PartitionSpec as P

MESH = pl.DeviceIdType.MESH
NX, NY, NZ = 4, 4, 8
TOK = 64
SUB = 896
DB = 256
DG = NX * DB
BLK = NX * TOK
Q = 16
NQ = TOK // Q
OWN = 2
R, L = 0, 1
F32, BF16 = jnp.float32, jnp.bfloat16


def kernel(
    g, gate, up, w, dw_out, gate_out, up_out,
    gate_v, up_v, hid, hh, gg, wg, part, rs_send, rs_recv, fin, fbuf, gate_f, up_f, acc, dws, land, x_land,
    act_sem, lsem, hs_s, hs_r, gx_s, gx_r, gy_s, gy_r, gc_s, gc_r, w_s, w_r,
    ag_s, ag_r, rs_s, rs_r, f_s, f_r, x_s, x_r, dw_s, dw_r,
):
    r, c = lax.axis_index("rows"), lax.axis_index("cols")
    y, core, x, z = r // 2, r % 2, c // NZ, c % NZ

    def dev(dx=0, dz=0, dy=0, dc=0):
        return (
            ((y + dy) % NY) * 2 + (core + dc) % 2,
            ((x + dx) % NX) * NZ + (z + dz + NZ) % NZ,
        )

    sent = []

    def send(src, dst, s, d, to):
        copy = pltpu.make_async_remote_copy(
            src_ref=src, dst_ref=dst, send_sem=s, recv_sem=d, device_id=to, device_id_type=MESH
        )
        copy.start()
        sent.append(copy)
        return copy

    def drain(count):
        for copy in sent[:count]:
            copy.wait_send()
        del sent[:count]

    def at(i, n):
        return pl.ds(pl.multiple_of(i * n, n), n)

    def lanes(i):
        return pl.ds(pl.multiple_of(i * SUB, 128), SUB)

    peers = [dev(dx=1), dev(dx=2), dev(dx=3), dev(dy=1), dev(dy=2), dev(dy=3), dev(dc=1), dev(dz=1), dev(dz=-1)]
    barrier = pltpu.get_barrier_semaphore()
    for peer in peers:
        pl.semaphore_signal(barrier, inc=1, device_id=peer, device_id_type=MESH)

    loads = {}
    for d in (0, 1, 3, 2):
        cols = lanes((x + d) % NX)
        for i, (src, dst) in enumerate(((gate, gate_v), (up, up_v))):
            loads[d, i] = pltpu.make_async_copy(src.at[:, cols], dst.at[:, cols], act_sem.at[d, i])
            loads[d, i].start()
    load_g = pltpu.make_async_copy(g, gg.at[at(core, 4), at(y, TOK), at(x, DB)], lsem.at[0])
    load_w = pltpu.make_async_copy(w.at[at(x, SUB)], wg.at[:, at(x, DB)], lsem.at[1])
    load_g.start()
    load_w.start()

    def hidden(d):
        loads[d, 0].wait()
        loads[d, 1].wait()
        cols = lanes((x + d) % NX)
        wide = gate_v[:, cols].astype(F32)
        swish = wide * jax.nn.sigmoid(wide)
        return (swish * up_v[:, cols].astype(F32)).astype(BF16)

    hh[z, at(x, TOK)] = hidden(0)
    pl.semaphore_wait(barrier, len(peers))

    ag = {}

    def last_hop(way, d):
        return 4 if (way == R) == (d < 2) else 3

    def gather(hop, d):
        src = (x + NX - d) % NX
        parts = OWN if d == 0 else 1
        n = TOK // parts
        for way in (R, L):
            for i in range(parts):
                j = i if d == 0 else OWN + d - 1
                if hop > 1 and hop - 1 <= last_hop(way, d):
                    ag[way, hop - 1, j].wait_recv()
                if hop <= last_hop(way, d):
                    b = (z - (hop - 1) + NZ) % NZ if way == R else (z + (hop - 1)) % NZ
                    piece = hh.at[b, pl.ds(pl.multiple_of(src * TOK + i * n, n), n)]
                    ag[way, hop, j] = send(
                        piece, piece, ag_s.at[way, hop - 1, j], ag_r.at[way, hop - 1, j], dev(dz=1 if way == R else -1)
                    )

    gather(1, 0)

    hid_copies = {}
    for d in (1, 3, 2):
        to = (x + d) % NX
        hid[to] = hidden(d)
        hid_copies[d] = send(hid.at[to], hh.at[z, at(x, TOK)], hs_s.at[d - 1], hs_r.at[d - 1], dev(dx=d))

    gy, gc = {}, []

    def rows_of(d, e, first=0, n=4):
        src = (x + NX - d) % NX
        return gg.at[pl.ds(core * 4 + first, n), at((y + NY - e) % NY, TOK), at(src, DB)]

    def to_sibling(d, i, piece):
        gc.append(send(piece, piece, gc_s.at[d, i], gc_r.at[d, i], dev(dc=1)))

    def spread(d):
        piece = rows_of(d, 0)
        for i, e in enumerate((1, 3)):
            gy[d, i] = send(piece, piece, gy_s.at[d, i], gy_r.at[d, i], dev(dy=e))
        to_sibling(d, 4, piece)

    def relay(d):
        for i, e in enumerate((1, 3)):
            gy[d, i].wait_recv()
            half = rows_of(d, e, 2 * i, 2)
            gy[d, 2 + i] = send(half, half, gy_s.at[d, 2 + i], gy_r.at[d, 2 + i], dev(dy=e))
            to_sibling(d, i, rows_of(d, e))

    def finish(d):
        for i in range(2):
            gy[d, 2 + i].wait_recv()
            to_sibling(d, 2 + i, rows_of(d, 2, 2 * i, 2))

    load_g.wait()
    spread(0)
    gather(2, 0)
    for d in (1, 3):
        hid_copies[d].wait_recv()
        gather(1, d)
    gx = {}
    for d in (1, 3, 2):
        gx[d] = send(g, gg.at[at(core, 4), at(y, TOK), at(x, DB)], gx_s.at[d - 1], gx_r.at[d - 1], dev(dx=d))
    hid_copies[2].wait_recv()
    gather(1, 2)
    w_copies = []
    for d in (1, 3, 2):
        to = (x + d) % NX
        w_copies.append(send(w.at[at(to, SUB)], wg.at[:, at(x, DB)], w_s.at[d - 1], w_r.at[d - 1], dev(dx=d)))
    relay(0)
    gather(2, 1)
    for d in (1, 3):
        gx[d].wait_recv()
        spread(d)
    gather(2, 3)
    gx[2].wait_recv()
    spread(2)
    gather(2, 2)

    for i in range(NX):
        cols = slice(i * SUB, (i + 1) * SUB)
        wide = gate_v[:, cols].astype(F32)
        sigmoid = jax.nn.sigmoid(wide)
        gate_f[:, cols] = up_v[:, cols].astype(F32) * sigmoid * (1.0 + wide * (1.0 - sigmoid))
        up_f[:, cols] = wide * sigmoid

    relay(1)
    gather(3, 0)
    relay(3)
    finish(0)
    gather(3, 1)
    relay(2)
    finish(1)
    gather(3, 3)
    finish(3)
    gather(3, 2)
    finish(2)
    for copy in gc:
        copy.wait_recv()

    def product(b):
        return lax.dot_general(hh[b], gg[b], (((0,), (0,)), ((), ())), preferred_element_type=F32)

    acc[...] = product(z)

    @pl.loop(0, 2)
    def _(i):
        acc[...] += product((z + 1 + 6 * i) % NZ)

    gather(4, 0)

    @pl.loop(0, 2)
    def _(i):
        acc[...] += product((z + 2 + 4 * i) % NZ)

    gather(4, 1)
    gather(4, 3)
    gather(4, 2)

    load_w.wait()
    for copy in w_copies:
        copy.wait_recv()

    def multiply(b):
        out = lax.dot_general(gg[b], wg[...], (((1,), (1,)), ((), ())), preferred_element_type=F32)
        part[b] = out.reshape(NX, TOK, SUB)

    rs = {}

    order = {
        R: ((1, 0), (3, 2, 1, 0), (3, 2, 0, 1), (2, 0)),
        L: ((2, 3), (1, 0, 2, 3), (1, 2, 0, 3), (2, 0)),
    }

    def running(way, step, k):
        b = (z + 4 - step) % NZ if way == R else (z + 4 + step) % NZ
        value = part[b, :, k * Q : (k + 1) * Q, :]
        if (way, step - 1, k) in rs:
            rs[way, step - 1, k].wait_recv()
            value = value + rs_recv[way, step - 1, k].astype(F32)
        return value.astype(BF16)

    def pass_on(way, step, k, src):
        rs[way, step, k] = send(
            src, rs_recv.at[way, step, k], rs_s.at[way, step, k], rs_r.at[way, step, k], dev(dz=1 if way == R else -1)
        )

    def reduce_both(step, places):
        for i in places:
            for way in (R, L):
                k = order[way][step][i]
                rs_send[way, step, k] = running(way, step, k)
                pass_on(way, step, k, rs_send.at[way, step, k])

    early, home = (3, 1), (2, 0)
    swapped = {}

    def swap(who, k, src):
        i = early.index(k)
        for d in (1, 3, 2):
            swapped[who, k, d] = send(
                src.at[(x + d) % NX], x_land.at[who, i, x], x_s.at[who, i, d - 1], x_r.at[who, i, d - 1], dev(dx=d)
            )
        x_land[who, i, x] = src[x]

    def wait_swap(who, k):
        for d in (1, 3, 2):
            swapped[who, k, d].wait_recv()

    multiply((z + 4) % NZ)
    reduce_both(0, (0, 1))
    multiply((z + 3) % NZ)
    multiply((z + 5) % NZ)
    reduce_both(1, (0, 1))

    @pl.loop(0, 2)
    def _(i):
        acc[...] += product((z + 3 + 2 * i) % NZ)

    multiply((z + 2) % NZ)
    multiply((z + 6) % NZ)

    for way, js in ((R, range(OWN + 1)), (L, (OWN + 2, OWN + 1))):
        for j in js:
            ag[way, 4, j].wait_recv()
    last = (z + 4) % NZ
    dw = {}
    for d in (1, 3, 2, 0):
        to = (x + d) % NX
        total = acc[:, at(to, DB)] + lax.dot_general(
            hh[last], gg[last, :, at(to, DB)], (((0,), (0,)), ((), ())), preferred_element_type=F32
        )
        if d == 0:
            dw_out[at(x, SUB)] = total
        else:
            dws[to] = total.astype(BF16)
            dw[d] = send(dws.at[to], land.at[x], dw_s.at[d - 1], dw_r.at[d - 1], dev(dx=d))

    before = len(sent) - 11
    reduce_both(1, (2, 3))

    @pl.loop(0, 3)
    def _(i):
        multiply((z + 7 + i) % NZ)

    drain(before)
    before = len(sent)
    reduce_both(2, (0, 1, 2, 3))
    drain(before)
    before = len(sent)
    def swap_running(pairs):
        for way, k in pairs:
            rs_send[way, 3, k] = running(way, 3, k)
            swap(way, k, rs_send.at[way, 3, k])

    swap_running(((R, 3), (L, 1)))
    reduce_both(3, (0, 1))
    swap_running(((R, 1), (L, 3)))
    for k in early:
        fin[k] = part[z, :, k * Q : (k + 1) * Q, :].astype(BF16)
        swap(2, k, fin.at[k])

    f = {}

    def give_back(k):
        i = home.index(k)
        value = part[z, :, k * Q : (k + 1) * Q, :]
        for way in (R, L):
            rs[way, 3, k].wait_recv()
            value = value + rs_recv[way, 3, k].astype(F32)
        fin[k] = value.astype(BF16)
        for d in (1, 3, 2):
            to = (x + d) % NX
            f[k, d] = send(fin.at[k, to], fbuf.at[i, x], f_s.at[i, d - 1], f_r.at[i, d - 1], dev(dx=d))
        fbuf[i, x] = fin[k, x]

    def last_step(pairs):
        for way, k in pairs:
            wait_swap(way, k)
            pass_on(way, 3, k, x_land.at[way, early.index(k)])

    last_step(((R, 3), (L, 1)))
    give_back(home[0])
    last_step(((R, 1), (L, 3)))
    give_back(home[1])
    drain(before)
    for d in (1, 3, 2):
        dw[d].wait_recv()
        src = (x + NX - d) % NX
        dw_out[at(src, SUB)] = land[src].astype(F32)

    def result(k, src, value):
        rows, cols = slice(k * Q, (k + 1) * Q), slice(src * SUB, (src + 1) * SUB)
        gate_out[rows, cols] = (value * gate_f[rows, cols]).astype(BF16)
        up_out[rows, cols] = (value * up_f[rows, cols]).astype(BF16)

    for i, k in enumerate(home):
        for d in (1, 3, 2):
            f[k, d].wait_recv()
        for src in range(NX):
            result(k, src, fbuf[i, src].astype(F32))
    for i, k in enumerate(early):
        wait_swap(2, k)
        for way in (R, L):
            rs[way, 3, k].wait_recv()
        for src in range(NX):
            value = x_land[2, i, src].astype(F32)
            for way in (R, L):
                value = value + rs_recv[way, 3, k, src].astype(F32)
            result(k, src, value)

    drain(len(sent))


def copy_out(*refs):
    ins, outs, sems = refs[:3], refs[3:6], refs[6]
    copies = [pltpu.make_async_copy(ins[i], outs[i], sems.at[i]) for i in range(3)]
    for copy in copies:
        copy.start()
    for copy in copies:
        copy.wait()


def shards(out_grad, gate_act, up_act, down_weight):
    dma = pltpu.SemaphoreType.DMA
    anywhere = pl.BlockSpec(memory_space=pl.ANY)
    in_vmem = pl.BlockSpec(memory_space=pltpu.VMEM)
    shapes = [((NX * SUB, DB), F32), ((TOK, NX * SUB), BF16), ((TOK, NX * SUB), BF16)]
    operands = (out_grad.reshape(4, TOK, DB), gate_act, up_act, down_weight)
    results = pl.pallas_call(
        kernel,
        out_shape=[pltpu.VMEM(*shape) for shape in shapes],
        in_specs=[anywhere] * 4,
        out_specs=[in_vmem] * 3,
        scratch_shapes=[
            pltpu.VMEM((TOK, NX * SUB), BF16),
            pltpu.VMEM((TOK, NX * SUB), BF16),
            pltpu.VMEM((NX, TOK, SUB), BF16),
            pltpu.VMEM((NZ, BLK, SUB), BF16),
            pltpu.VMEM((NZ, BLK, DG), BF16),
            pltpu.VMEM((SUB, DG), BF16),
            pltpu.VMEM((NZ, NX, TOK, SUB), F32),
            pltpu.VMEM((2, 4, NQ, NX, Q, SUB), BF16),
            pltpu.VMEM((2, 4, NQ, NX, Q, SUB), BF16),
            pltpu.VMEM((NQ, NX, Q, SUB), BF16),
            pltpu.VMEM((2, NX, Q, SUB), BF16),
            pltpu.VMEM((TOK, NX * SUB), F32),
            pltpu.VMEM((TOK, NX * SUB), F32),
            pltpu.VMEM((SUB, DG), F32),
            pltpu.VMEM((NX, SUB, DB), BF16),
            pltpu.VMEM((NX, SUB, DB), BF16),
            pltpu.VMEM((3, 2, NX, Q, SUB), BF16),
            dma((4, 2)), dma((2,)),
            dma((3,)), dma((3,)),
            dma((3,)), dma((3,)),
            dma((4, 4)), dma((4, 4)),
            dma((4, 5)), dma((4, 5)),
            dma((3,)), dma((3,)),
            dma((2, 4, OWN + 3)), dma((2, 4, OWN + 3)),
            dma((2, 4, NQ)), dma((2, 4, NQ)),
            dma((2, 3)), dma((2, 3)),
            dma((3, 2, 3)), dma((3, 2, 3)),
            dma((3,)), dma((3,)),
        ],
        compiler_params=pltpu.CompilerParams(
            collective_id=0, has_side_effects=True, vmem_limit_bytes=50 << 20
        ),
    )(*[pltpu.with_memory_space_constraint(operand, pltpu.HBM) for operand in operands])
    return pl.pallas_call(
        copy_out,
        out_shape=[jax.ShapeDtypeStruct(*shape) for shape in shapes],
        in_specs=[anywhere] * 3,
        out_specs=[anywhere] * 3,
        scratch_shapes=[dma((3,))],
        compiler_params=pltpu.CompilerParams(vmem_limit_bytes=1 << 20),
    )(*[pltpu.with_memory_space_constraint(result, pltpu.VMEM) for result in results])


def solution(mesh):
    in_specs = (P("rows", "cols"), P("cols", "rows"), P("cols", "rows"), P("rows", "cols"))
    out_specs = (P("rows", "cols"), P("cols", "rows"), P("cols", "rows"))
    return jax.shard_map(shards, mesh=mesh, in_specs=in_specs, out_specs=out_specs, check_vma=False)
```

```python
import jax
import jax.numpy as jnp
from jax import lax
from jax.experimental import pallas as pl
from jax.experimental.pallas import tpu as pltpu
from jax.sharding import PartitionSpec as P

MESH = pl.DeviceIdType.MESH
NX, NY, NZ = 4, 4, 8
TOK = 64
SUB = 896
DB = 256
DG = NX * DB
BLK = NX * TOK
Q = 16
NQ = TOK // Q
OWN = 2
R, L = 0, 1
F32, BF16 = jnp.float32, jnp.bfloat16


def kernel(
    g, gate, up, w, dw_out, gate_out, up_out,
    gate_v, up_v, hid, hh, gg, wg, part, rs_send, rs_recv, fin, fbuf, gate_f, up_f, acc, dws, land, x_land,
    act_sem, lsem, hs_s, hs_r, gx_s, gx_r, gy_s, gy_r, gc_s, gc_r, w_s, w_r,
    ag_s, ag_r, rs_s, rs_r, f_s, f_r, x_s, x_r, dw_s, dw_r,
):
    r, c = lax.axis_index("rows"), lax.axis_index("cols")
    y, core, x, z = r // 2, r % 2, c // NZ, c % NZ

    def dev(dx=0, dz=0, dy=0, dc=0):
        return (
            ((y + dy) % NY) * 2 + (core + dc) % 2,
            ((x + dx) % NX) * NZ + (z + dz + NZ) % NZ,
        )

    sent = []

    def send(src, dst, s, d, to):
        copy = pltpu.make_async_remote_copy(
            src_ref=src, dst_ref=dst, send_sem=s, recv_sem=d, device_id=to, device_id_type=MESH
        )
        copy.start()
        sent.append(copy)
        return copy

    def drain(count):
        for copy in sent[:count]:
            copy.wait_send()
        del sent[:count]

    def at(i, n):
        return pl.ds(pl.multiple_of(i * n, n), n)

    def lanes(i):
        return pl.ds(pl.multiple_of(i * SUB, 128), SUB)

    peers = [dev(dx=1), dev(dx=2), dev(dx=3), dev(dy=1), dev(dy=2), dev(dy=3), dev(dc=1), dev(dz=1), dev(dz=-1)]
    barrier = pltpu.get_barrier_semaphore()
    for peer in peers:
        pl.semaphore_signal(barrier, inc=1, device_id=peer, device_id_type=MESH)

    loads = {}
    for d in (0, 1, 3, 2):
        cols = lanes((x + d) % NX)
        for i, (src, dst) in enumerate(((gate, gate_v), (up, up_v))):
            loads[d, i] = pltpu.make_async_copy(src.at[:, cols], dst.at[:, cols], act_sem.at[d, i])
            loads[d, i].start()
    load_g = pltpu.make_async_copy(g, gg.at[at(core, 4), at(y, TOK), at(x, DB)], lsem.at[0])
    load_w = pltpu.make_async_copy(w.at[at(x, SUB)], wg.at[:, at(x, DB)], lsem.at[1])
    load_g.start()
    load_w.start()

    def hidden(d):
        loads[d, 0].wait()
        loads[d, 1].wait()
        cols = lanes((x + d) % NX)
        wide = gate_v[:, cols].astype(F32)
        swish = wide * jax.nn.sigmoid(wide)
        return (swish * up_v[:, cols].astype(F32)).astype(BF16)

    hh[z, at(x, TOK)] = hidden(0)
    pl.semaphore_wait(barrier, len(peers))

    ag = {}

    def last_hop(way, d):
        return 4 if (way == R) == (d < 2) else 3

    def gather(hop, d):
        src = (x + NX - d) % NX
        parts = OWN if d == 0 else 1
        n = TOK // parts
        for way in (R, L):
            for i in range(parts):
                j = i if d == 0 else OWN + d - 1
                if hop > 1 and hop - 1 <= last_hop(way, d):
                    ag[way, hop - 1, j].wait_recv()
                if hop <= last_hop(way, d):
                    b = (z - (hop - 1) + NZ) % NZ if way == R else (z + (hop - 1)) % NZ
                    piece = hh.at[b, pl.ds(pl.multiple_of(src * TOK + i * n, n), n)]
                    ag[way, hop, j] = send(
                        piece, piece, ag_s.at[way, hop - 1, j], ag_r.at[way, hop - 1, j], dev(dz=1 if way == R else -1)
                    )

    gather(1, 0)

    hid_copies = {}
    for d in (1, 3, 2):
        to = (x + d) % NX
        hid[to] = hidden(d)
        hid_copies[d] = send(hid.at[to], hh.at[z, at(x, TOK)], hs_s.at[d - 1], hs_r.at[d - 1], dev(dx=d))

    gy, gc = {}, []

    def rows_of(d, e, first=0, n=4):
        src = (x + NX - d) % NX
        return gg.at[pl.ds(core * 4 + first, n), at((y + NY - e) % NY, TOK), at(src, DB)]

    def to_sibling(d, i, piece):
        gc.append(send(piece, piece, gc_s.at[d, i], gc_r.at[d, i], dev(dc=1)))

    def spread(d):
        piece = rows_of(d, 0)
        for i, e in enumerate((1, 3)):
            gy[d, i] = send(piece, piece, gy_s.at[d, i], gy_r.at[d, i], dev(dy=e))
        to_sibling(d, 4, piece)

    def relay(d):
        for i, e in enumerate((1, 3)):
            gy[d, i].wait_recv()
            half = rows_of(d, e, 2 * i, 2)
            gy[d, 2 + i] = send(half, half, gy_s.at[d, 2 + i], gy_r.at[d, 2 + i], dev(dy=e))
            to_sibling(d, i, rows_of(d, e))

    def finish(d):
        for i in range(2):
            gy[d, 2 + i].wait_recv()
            to_sibling(d, 2 + i, rows_of(d, 2, 2 * i, 2))

    load_g.wait()
    spread(0)
    gather(2, 0)
    for d in (1, 3):
        hid_copies[d].wait_recv()
        gather(1, d)
    gx = {}
    for d in (1, 3, 2):
        gx[d] = send(g, gg.at[at(core, 4), at(y, TOK), at(x, DB)], gx_s.at[d - 1], gx_r.at[d - 1], dev(dx=d))
    hid_copies[2].wait_recv()
    gather(1, 2)
    w_copies = []
    for d in (1, 3, 2):
        to = (x + d) % NX
        w_copies.append(send(w.at[at(to, SUB)], wg.at[:, at(x, DB)], w_s.at[d - 1], w_r.at[d - 1], dev(dx=d)))
    relay(0)
    gather(2, 1)
    for d in (1, 3):
        gx[d].wait_recv()
        spread(d)
    gather(2, 3)
    gx[2].wait_recv()
    spread(2)
    gather(2, 2)

    for i in range(NX):
        cols = slice(i * SUB, (i + 1) * SUB)
        wide = gate_v[:, cols].astype(F32)
        sigmoid = jax.nn.sigmoid(wide)
        gate_f[:, cols] = up_v[:, cols].astype(F32) * sigmoid * (1.0 + wide * (1.0 - sigmoid))
        up_f[:, cols] = wide * sigmoid

    relay(1)
    gather(3, 0)
    relay(3)
    finish(0)
    gather(3, 1)
    relay(2)
    finish(1)
    gather(3, 3)
    finish(3)
    gather(3, 2)
    finish(2)
    for copy in gc:
        copy.wait_recv()

    def product(b):
        return lax.dot_general(hh[b], gg[b], (((0,), (0,)), ((), ())), preferred_element_type=F32)

    acc[...] = product(z)

    @pl.loop(0, 2)
    def _(i):
        acc[...] += product((z + 1 + 6 * i) % NZ)

    gather(4, 0)

    @pl.loop(0, 2)
    def _(i):
        acc[...] += product((z + 2 + 4 * i) % NZ)

    gather(4, 1)
    gather(4, 3)
    gather(4, 2)

    load_w.wait()
    for copy in w_copies:
        copy.wait_recv()

    def multiply(b):
        out = lax.dot_general(gg[b], wg[...], (((1,), (1,)), ((), ())), preferred_element_type=F32)
        part[b] = out.reshape(NX, TOK, SUB)

    rs = {}

    order = {
        R: ((1, 0), (3, 2, 1, 0), (3, 2, 0, 1), (2, 0)),
        L: ((2, 3), (1, 0, 2, 3), (1, 2, 0, 3), (2, 0)),
    }

    def running(way, step, k):
        b = (z + 4 - step) % NZ if way == R else (z + 4 + step) % NZ
        value = part[b, :, k * Q : (k + 1) * Q, :]
        if (way, step - 1, k) in rs:
            rs[way, step - 1, k].wait_recv()
            value = value + rs_recv[way, step - 1, k].astype(F32)
        return value.astype(BF16)

    def pass_on(way, step, k, src):
        rs[way, step, k] = send(
            src, rs_recv.at[way, step, k], rs_s.at[way, step, k], rs_r.at[way, step, k], dev(dz=1 if way == R else -1)
        )

    def reduce_both(step, places):
        for i in places:
            for way in (R, L):
                k = order[way][step][i]
                rs_send[way, step, k] = running(way, step, k)
                pass_on(way, step, k, rs_send.at[way, step, k])

    early, home = (3, 1), (2, 0)
    swapped = {}

    def swap(who, k, src):
        i = early.index(k)
        for d in (1, 3, 2):
            swapped[who, k, d] = send(
                src.at[(x + d) % NX], x_land.at[who, i, x], x_s.at[who, i, d - 1], x_r.at[who, i, d - 1], dev(dx=d)
            )
        x_land[who, i, x] = src[x]

    def wait_swap(who, k):
        for d in (1, 3, 2):
            swapped[who, k, d].wait_recv()

    multiply((z + 4) % NZ)
    reduce_both(0, (0, 1))
    multiply((z + 3) % NZ)
    multiply((z + 5) % NZ)
    reduce_both(1, (0, 1))

    @pl.loop(0, 2)
    def _(i):
        acc[...] += product((z + 3 + 2 * i) % NZ)

    for way, js in ((R, range(OWN + 1)), (L, (OWN + 2, OWN + 1))):
        for j in js:
            ag[way, 4, j].wait_recv()
    last = (z + 4) % NZ
    dw = {}
    for d in (1, 3, 2, 0):
        to = (x + d) % NX
        total = acc[:, at(to, DB)] + lax.dot_general(
            hh[last], gg[last, :, at(to, DB)], (((0,), (0,)), ((), ())), preferred_element_type=F32
        )
        if d == 0:
            dw_out[at(x, SUB)] = total
        else:
            dws[to] = total.astype(BF16)
            dw[d] = send(dws.at[to], land.at[x], dw_s.at[d - 1], dw_r.at[d - 1], dev(dx=d))

    before = len(sent) - 11
    multiply((z + 2) % NZ)
    multiply((z + 6) % NZ)
    reduce_both(1, (2, 3))

    @pl.loop(0, 3)
    def _(i):
        multiply((z + 7 + i) % NZ)

    drain(before)
    before = len(sent)
    reduce_both(2, (0, 1, 2, 3))
    drain(before)
    before = len(sent)
    def swap_running(pairs):
        for way, k in pairs:
            rs_send[way, 3, k] = running(way, 3, k)
            swap(way, k, rs_send.at[way, 3, k])

    swap_running(((R, 3), (L, 1)))
    reduce_both(3, (0, 1))
    swap_running(((R, 1), (L, 3)))
    for k in early:
        fin[k] = part[z, :, k * Q : (k + 1) * Q, :].astype(BF16)
        swap(2, k, fin.at[k])

    f = {}

    def give_back(k):
        i = home.index(k)
        value = part[z, :, k * Q : (k + 1) * Q, :]
        for way in (R, L):
            rs[way, 3, k].wait_recv()
            value = value + rs_recv[way, 3, k].astype(F32)
        fin[k] = value.astype(BF16)
        for d in (1, 3, 2):
            to = (x + d) % NX
            f[k, d] = send(fin.at[k, to], fbuf.at[i, x], f_s.at[i, d - 1], f_r.at[i, d - 1], dev(dx=d))
        fbuf[i, x] = fin[k, x]

    def last_step(pairs):
        for way, k in pairs:
            wait_swap(way, k)
            pass_on(way, 3, k, x_land.at[way, early.index(k)])

    last_step(((R, 3), (L, 1)))
    give_back(home[0])
    last_step(((R, 1), (L, 3)))
    give_back(home[1])
    drain(before)
    for d in (1, 3, 2):
        dw[d].wait_recv()
        src = (x + NX - d) % NX
        dw_out[at(src, SUB)] = land[src].astype(F32)

    def result(k, src, value):
        rows, cols = slice(k * Q, (k + 1) * Q), slice(src * SUB, (src + 1) * SUB)
        gate_out[rows, cols] = (value * gate_f[rows, cols]).astype(BF16)
        up_out[rows, cols] = (value * up_f[rows, cols]).astype(BF16)

    for i, k in enumerate(home):
        for d in (1, 3, 2):
            f[k, d].wait_recv()
        for src in range(NX):
            result(k, src, fbuf[i, src].astype(F32))
    for i, k in enumerate(early):
        wait_swap(2, k)
        for way in (R, L):
            rs[way, 3, k].wait_recv()
        for src in range(NX):
            value = x_land[2, i, src].astype(F32)
            for way in (R, L):
                value = value + rs_recv[way, 3, k, src].astype(F32)
            result(k, src, value)

    drain(len(sent))


def copy_out(*refs):
    ins, outs, sems = refs[:3], refs[3:6], refs[6]
    copies = [pltpu.make_async_copy(ins[i], outs[i], sems.at[i]) for i in range(3)]
    for copy in copies:
        copy.start()
    for copy in copies:
        copy.wait()


def shards(out_grad, gate_act, up_act, down_weight):
    dma = pltpu.SemaphoreType.DMA
    anywhere = pl.BlockSpec(memory_space=pl.ANY)
    in_vmem = pl.BlockSpec(memory_space=pltpu.VMEM)
    shapes = [((NX * SUB, DB), F32), ((TOK, NX * SUB), BF16), ((TOK, NX * SUB), BF16)]
    operands = (out_grad.reshape(4, TOK, DB), gate_act, up_act, down_weight)
    results = pl.pallas_call(
        kernel,
        out_shape=[pltpu.VMEM(*shape) for shape in shapes],
        in_specs=[anywhere] * 4,
        out_specs=[in_vmem] * 3,
        scratch_shapes=[
            pltpu.VMEM((TOK, NX * SUB), BF16),
            pltpu.VMEM((TOK, NX * SUB), BF16),
            pltpu.VMEM((NX, TOK, SUB), BF16),
            pltpu.VMEM((NZ, BLK, SUB), BF16),
            pltpu.VMEM((NZ, BLK, DG), BF16),
            pltpu.VMEM((SUB, DG), BF16),
            pltpu.VMEM((NZ, NX, TOK, SUB), F32),
            pltpu.VMEM((2, 4, NQ, NX, Q, SUB), BF16),
            pltpu.VMEM((2, 4, NQ, NX, Q, SUB), BF16),
            pltpu.VMEM((NQ, NX, Q, SUB), BF16),
            pltpu.VMEM((2, NX, Q, SUB), BF16),
            pltpu.VMEM((TOK, NX * SUB), F32),
            pltpu.VMEM((TOK, NX * SUB), F32),
            pltpu.VMEM((SUB, DG), F32),
            pltpu.VMEM((NX, SUB, DB), BF16),
            pltpu.VMEM((NX, SUB, DB), BF16),
            pltpu.VMEM((3, 2, NX, Q, SUB), BF16),
            dma((4, 2)), dma((2,)),
            dma((3,)), dma((3,)),
            dma((3,)), dma((3,)),
            dma((4, 4)), dma((4, 4)),
            dma((4, 5)), dma((4, 5)),
            dma((3,)), dma((3,)),
            dma((2, 4, OWN + 3)), dma((2, 4, OWN + 3)),
            dma((2, 4, NQ)), dma((2, 4, NQ)),
            dma((2, 3)), dma((2, 3)),
            dma((3, 2, 3)), dma((3, 2, 3)),
            dma((3,)), dma((3,)),
        ],
        compiler_params=pltpu.CompilerParams(
            collective_id=0, has_side_effects=True, vmem_limit_bytes=50 << 20
        ),
    )(*[pltpu.with_memory_space_constraint(operand, pltpu.HBM) for operand in operands])
    return pl.pallas_call(
        copy_out,
        out_shape=[jax.ShapeDtypeStruct(*shape) for shape in shapes],
        in_specs=[anywhere] * 3,
        out_specs=[anywhere] * 3,
        scratch_shapes=[dma((3,))],
        compiler_params=pltpu.CompilerParams(vmem_limit_bytes=1 << 20),
    )(*[pltpu.with_memory_space_constraint(result, pltpu.VMEM) for result in results])


def solution(mesh):
    in_specs = (P("rows", "cols"), P("cols", "rows"), P("cols", "rows"), P("rows", "cols"))
    out_specs = (P("rows", "cols"), P("cols", "rows"), P("cols", "rows"))
    return jax.shard_map(shards, mesh=mesh, in_specs=in_specs, out_specs=out_specs, check_vma=False)
```
